1024 devices in a mesh: wide: 32 (over z, core), group: 32 (over x, y).
Axes of the slice: x: 4, y: 8, z: 16, core: 2. Of those that a mesh axis runs over, the one named last changes fastest.
Arguments:
- patches: bfloat16 [16384, 16, 1152], P(('wide', 'group')), may hold values from -6 to 6
- counts: int32 [16384], P(('wide', 'group')), may hold values from 4 to 16, as said below
- key_weight: bfloat16 [1152, 1152], replicated, may hold values from -0.1875 to 0.1875
- value_weight: bfloat16 [1152, 1152], replicated, may hold values from -0.1875 to 0.1875
- probe_query: bfloat16 [16, 72], replicated, may hold values from -5 to 5
- text_embed: bfloat16 [16384, 1152], P(('wide', 'group')), may hold values from -6 to 6
- labels: int32 [16384], P(('wide', 'group')), may hold values from 0 to 511
- logit_scale: float32 [], replicated, may hold values from 4 to 16
- logit_bias: float32 [], replicated, may hold values from -6 to -2
Outputs:
- row_loss: float32 [16384], P(('wide', 'group'))
- text_grad: float32 [16384, 1152], P(('wide', 'group'))
The draws below stay inside these ranges and needn't reach their ends.
Inputs may be any that keep to these rules, and one draw needn't show every extreme that they name: `counts`: counts come in blocks of 16 images. Among the 32 blocks b with the same b // 32, exactly 8 hold only images of 16 patches; every other block's images have 4 or 6 patches, 16 * (5) patches in all.
All inputs are finite; a program needn't handle non-finite values.
Results may differ from the reference program's by a relative error of at most 0.0085.
Values may be sent and summed in bfloat16 or wider, within the bound.
No kernel may reach another device: no remote copies, remote signals or barrier semaphores. Data moves between devices by JAX's collectives and lax.ppermute only.
A program may use at most 32 MiB of HBM per device.

```python
import math
import jax
import jax.numpy as jnp
from jax import lax

D = 1152
HEADS = 16
HEAD_DIM = 72
MAXP = 16
MINP = 4
IMG_DEV = 16
BATCH = 512
IMAGES = 16384
N_WIDE = 32
N_GROUP = 32


def draw_counts(key, part):
    key = jax.random.fold_in(key, 7)
    line_key = jax.random.fold_in(key, 1)
    image_key = jax.random.fold_in(key, 2)
    line_keys = jax.random.split(line_key, N_WIDE)
    places = jax.vmap(lambda k: jax.random.permutation(k, N_GROUP))(line_keys)
    heavy = (places < N_GROUP // 4).reshape(N_WIDE * N_GROUP, 1)
    block_keys = jax.random.split(image_key, N_WIDE * N_GROUP)
    orders = jax.vmap(lambda k: jax.random.permutation(k, IMG_DEV))(block_keys)
    light = MINP + 2 * (orders % 2)
    result = jnp.where(heavy, MAXP, light)
    return result.reshape(IMAGES).astype(jnp.int32)


def plant(entries, own_key, least, top_value):
    index_at = [jax.random.randint(jax.random.fold_in(own_key, axis), (), 0, length) for axis, length in enumerate(entries.shape)]
    widest = entries.shape.index(max(entries.shape))
    neighbour = index_at[:widest] + [(index_at[widest] + 1) % entries.shape[widest]] + index_at[widest + 1:]
    return entries.at[tuple(index_at)].set(least).at[tuple(neighbour)].set(top_value)


def levels(rng, extent, cuts, least, high):
    def one(dim, shards_of):
        draws = jax.random.uniform(jax.random.fold_in(jax.random.fold_in(rng, 6), dim), (shards_of,), jnp.float32, least / len(cuts), high / len(cuts))
        return jnp.repeat(jnp.exp(draws), extent[dim] // shards_of).reshape((-1,) + (1,) * (len(extent) - dim - 1))

    level = one(*cuts[0])
    for cut in cuts[1:]:
        level = level * one(*cut)
    return level


def bell_draw(key, dims, spread, most, cuts=(), dtype=jnp.bfloat16):
    gain = levels(key, dims, cuts, -0.22, 0.18) if cuts else 1.0
    values = jax.random.normal(key, dims, jnp.float32) * spread * gain
    return jnp.minimum(jnp.maximum(values, -most), most).astype(dtype)


def setup_inputs(seed: int = 0) -> dict:
    keys = jax.random.split(jax.random.key(seed), 10)
    patches = bell_draw(keys[0], (IMAGES, MAXP, D), 1.0, 6.0, ((0, 1024),))
    counts = draw_counts(jax.random.fold_in(keys[9], 71), 0)
    key_weight = bell_draw(keys[2], (D, D), D ** -0.5, 0.1875)
    value_weight = bell_draw(keys[3], (D, D), D ** -0.5, 0.1875)
    probe_query = bell_draw(keys[4], (HEADS, HEAD_DIM), 1.0, 5.0)
    text_embed = bell_draw(keys[5], (IMAGES, D), 1.0, 6.0, ((0, 1024),))
    labels = plant(jax.random.randint(keys[6], (IMAGES,), 0, BATCH), jax.random.fold_in(keys[6], 1), 0, BATCH - 1).astype(jnp.int32)
    logit_scale = jnp.clip(jnp.exp(jax.random.uniform(keys[7], (), jnp.float32, math.log(4.0), math.log(16.0))), 4.0, 16.0)
    logit_bias = jnp.clip(jax.random.uniform(keys[8], (), jnp.float32, -6.0, -2.0), -6.0, -2.0)
    return {"patches": patches, "counts": counts, "key_weight": key_weight, "value_weight": value_weight, "probe_query": probe_query, "text_embed": text_embed, "labels": labels, "logit_scale": logit_scale, "logit_bias": logit_bias}


def pool_rows(patch_rows, patch_counts, key_weight, value_weight, probe_query):
    lead_dims = patch_rows.shape[:-2]
    patch_count = patch_rows.shape[-2]
    model_width = patch_rows.shape[-1]
    head_count = probe_query.shape[0]
    head_size = probe_query.shape[1]
    flat_rows = patch_rows.reshape(-1, model_width)
    key_rows = jnp.dot(flat_rows, key_weight, preferred_element_type=jnp.float32).astype(jnp.bfloat16)
    value_rows = jnp.dot(flat_rows, value_weight, preferred_element_type=jnp.float32).astype(jnp.bfloat16)
    key_rows = key_rows.reshape(-1, patch_count, head_count, head_size)
    value_rows = value_rows.reshape(-1, patch_count, head_count, head_size)
    scores = jnp.einsum('rphe,he->rhp', key_rows.astype(jnp.float32), probe_query.astype(jnp.float32))
    scores = scores * (1.0 / head_size ** 0.5)
    is_valid = lax.broadcasted_iota(jnp.int32, (1, 1, patch_count), 2) < patch_counts.reshape(-1, 1, 1)
    scores = jnp.where(is_valid, scores, -1e+30)
    attend = jax.nn.softmax(scores, axis=-1).astype(jnp.bfloat16)
    pooled = jnp.einsum('rhp,rphe->rhe', attend.astype(jnp.float32), value_rows.astype(jnp.float32))
    return pooled.reshape(lead_dims + (model_width,)).astype(jnp.bfloat16)

def unit_rows(embed):
    embed32 = embed.astype(jnp.float32)
    length = jnp.sqrt(lax.optimization_barrier(jnp.sum(embed32 * embed32, axis=-1, keepdims=True)) + 1e-06)
    return (embed32 / length, length)

def by_batch(array):
    tail = array.shape[1:]
    blocks = array.reshape((N_WIDE, N_GROUP, IMG_DEV) + tail)
    blocks = jnp.moveaxis(blocks, 1, 0)
    return blocks.reshape((N_GROUP, N_WIDE * IMG_DEV) + tail)

def from_batch(array):
    tail = array.shape[2:]
    blocks = array.reshape((N_GROUP, N_WIDE, IMG_DEV) + tail)
    blocks = jnp.moveaxis(blocks, 0, 1)
    return blocks.reshape((N_WIDE * N_GROUP * IMG_DEV,) + tail)

def reference(patches, counts, key_weight, value_weight, probe_query, text_embed, labels, logit_scale, logit_bias):
    block_rows = patches.reshape(IMAGES // IMG_DEV, IMG_DEV, MAXP, D)
    block_counts = counts.reshape(IMAGES // IMG_DEV, IMG_DEV)
    pooled = lax.map(lambda pair: pool_rows(pair[0], pair[1], key_weight, value_weight, probe_query), (block_rows, block_counts))
    pooled = pooled.reshape(IMAGES, D)
    image_dir, image_length = unit_rows(pooled)
    image_unit = image_dir.astype(jnp.bfloat16)
    unit, text_length = unit_rows(text_embed)
    text_unit = unit.astype(jnp.bfloat16)
    image_batch = by_batch(image_unit).astype(jnp.float32)
    text_batch = by_batch(text_unit).astype(jnp.float32)
    label_batch = by_batch(labels)
    logits = logit_scale * jnp.einsum('gid,gjd->gij', image_batch, text_batch) + logit_bias
    column = lax.broadcasted_iota(jnp.int32, (1, 1, BATCH), 2)
    signs = jnp.where(column == label_batch[:, :, None], 1.0, -1.0).astype(jnp.float32)
    row_loss = lax.optimization_barrier(jnp.sum(jax.nn.softplus(-signs * logits), axis=-1))
    slope = -signs * jax.nn.sigmoid(-signs * logits)
    unit_grad = logit_scale * jnp.einsum('gij,gid->gjd', slope, image_batch, precision=lax.Precision.HIGHEST)
    unit_grad = from_batch(unit_grad)
    along = lax.optimization_barrier(jnp.sum(unit_grad * unit, axis=-1, keepdims=True))
    text_grad = (unit_grad - along * unit) / text_length
    return (from_batch(row_loss), text_grad)
```

```python
import functools

import jax
import jax.numpy as jnp
from jax import lax
from jax.experimental import pallas as pl
from jax.experimental.pallas import tpu as pltpu
from jax.sharding import PartitionSpec as P

LANES = 128
NEAR = 4
CHUNKS = 3

VMEM = pl.BlockSpec(memory_space=pltpu.VMEM)
SMEM = pl.BlockSpec(memory_space=pltpu.SMEM)
ANY = pl.BlockSpec(memory_space=pl.ANY)


def dot(left, right):
    return jnp.dot(left, right, preferred_element_type=jnp.float32)


def row_dot(left, right):
    return lax.dot_general(
        left, right, (((1,), (1,)), ((), ())), preferred_element_type=jnp.float32
    )


def iota(shape, dim):
    return lax.broadcasted_iota(jnp.int32, shape, dim)


def pool_kernel(
    text_hbm, query_hbm, patches_hbm, key_hbm, value_hbm, counts_ref, labels_ref,
    out_ref, text_ref, query_ref, patches_ref, key_ref, value_ref, sems,
):
    images, patch_count, width = patches_ref.shape
    heads, head_size = query_ref.shape
    rows = images * patch_count
    block = width // CHUNKS
    copies = []

    def fetch(source, target):
        copies.append(pltpu.make_async_copy(source, target, sems.at[len(copies)]))
        copies[-1].start()

    fetch(patches_hbm, patches_ref)
    for source, target in ((key_hbm, key_ref), (value_hbm, value_ref)):
        for c in range(CHUNKS):
            at = pl.ds(c * block, block)
            fetch(source.at[:, at], target.at[:, at])
            if len(copies) == 2:
                fetch(text_hbm, text_ref)
                fetch(query_hbm, query_ref)
    patches_copy, text_copy, query_copy = copies[0], copies[2], copies[3]
    copies = copies[1:2] + copies[4:]

    text_copy.wait()
    text = text_ref[...].astype(jnp.float32)
    length = jnp.sqrt(jnp.sum(text * text, axis=-1, keepdims=True) + 1e-06)
    out_ref[0:images, 0:width] = (text / length).astype(jnp.bfloat16)
    wide = lax.axis_index("wide")
    lane = iota((images, LANES), 1)
    row = iota((images, LANES), 0)
    place = (lane == wide) | (lane == row + 32)
    out_ref[0:images, width:] = jnp.where(place, 1.0, 0.0).astype(jnp.bfloat16)
    first = jnp.zeros((images, LANES), jnp.int32)
    second = jnp.zeros((images, LANES), jnp.int32)
    valid = jnp.zeros((images, patch_count, heads), jnp.int32)
    image = iota((images, patch_count, heads), 0)
    for i in range(images):
        label = labels_ref[i]
        high = lax.shift_right_logical(label, 4)
        first = jnp.where(row == i, high, first)
        second = jnp.where(row == i, label - 16 * high + 32, second)
        valid = jnp.where(image == i, counts_ref[i], valid)
    place = (lane == first) | (lane == second)
    out_ref[images:, width:] = jnp.where(place, 1.0, 0.0).astype(jnp.bfloat16)

    column = iota((1, width), 1)
    head_of = jnp.zeros((1, width), jnp.int32)
    for h in range(1, heads):
        head_of += (column >= h * head_size).astype(jnp.int32)
    inner = column - head_of * head_size
    query_copy.wait()
    spread = jnp.where(iota((head_size, width), 0) == inner, 1.0, 0.0).astype(jnp.bfloat16)
    own = iota((heads, width), 0) == head_of
    query = jnp.where(own, dot(query_ref[...], spread), 0.0).astype(jnp.bfloat16)
    own = jnp.where(own, 1.0, 0.0).astype(jnp.bfloat16)

    patches_copy.wait()
    flat = patches_ref[...].reshape(rows, width)
    scores = jnp.zeros((rows, heads), jnp.float32)
    for c in range(CHUNKS):
        copies[c].wait()
        at = slice(c * block, (c + 1) * block)
        keys = dot(flat, key_ref[:, at]).astype(jnp.bfloat16)
        scores += row_dot(keys, query[:, at])
    scores = (scores * (1.0 / head_size**0.5)).reshape(images, patch_count, heads)
    scores = jnp.where(iota((images, patch_count, heads), 1) < valid, scores, -1e30)
    scores = jnp.exp(scores - jnp.max(scores, axis=1, keepdims=True))
    attend = scores / jnp.sum(scores, axis=1, keepdims=True)
    attend = attend.reshape(rows, heads).astype(jnp.bfloat16)
    pooled = []
    for c in range(CHUNKS):
        copies[CHUNKS + c].wait()
        at = slice(c * block, (c + 1) * block)
        values = dot(flat, value_ref[:, at]).astype(jnp.bfloat16).astype(jnp.float32)
        terms = dot(attend, own[:, at]) * values
        terms = jnp.sum(terms.reshape(images, patch_count, block), axis=1)
        pooled.append(terms.astype(jnp.bfloat16).astype(jnp.float32))
    square = sum(jnp.sum(p * p, axis=-1, keepdims=True) for p in pooled)
    length = jnp.sqrt(square + 1e-06)
    for c in range(CHUNKS):
        at = slice(c * block, (c + 1) * block)
        out_ref[images:, at] = (pooled[c] / length).astype(jnp.bfloat16)


def pair_kernel(
    images, near_ref, far_ref, scale_hbm, bias_hbm, out_ref, scale_ref, bias_ref, sems
):
    near, width = near_ref.shape[0], near_ref.shape[1] - LANES
    far = far_ref.shape[0]
    copies = [
        pltpu.make_async_copy(scale_hbm, scale_ref, sems.at[0]),
        pltpu.make_async_copy(bias_hbm, bias_ref, sems.at[1]),
    ]
    for copy in copies:
        copy.start()
    raw = row_dot(near_ref[:, :width], far_ref[:, :width])
    match = row_dot(near_ref[:, width:], far_ref[:, width:])
    sign = jnp.where(match > 1.5, 1.0, -1.0)
    for copy in copies:
        copy.wait()
    scale, bias = scale_ref[0], bias_ref[0]
    logits = -sign * (scale * raw + bias)
    small = jnp.exp(-jnp.abs(logits))
    softplus = jnp.maximum(logits, 0.0) + jnp.log1p(small)
    slope = -sign * (jnp.where(logits >= 0.0, 1.0, small) / (1.0 + small))
    far_is_text = (iota((near, far), 1) & images) == 0
    loss = jnp.sum(jnp.where(far_is_text, softplus, 0.0), axis=-1, keepdims=True)
    slope = jnp.where(far_is_text, 0.0, slope)
    blocks = near // (2 * images)
    slope = slope.reshape(blocks, 2 * images, far)[:, :images].reshape(blocks * images, far)
    loss = loss.reshape(blocks, 2 * images, 1)[:, images:].reshape(blocks * images, 1)
    high = slope.astype(jnp.bfloat16)
    low = (slope - high.astype(jnp.float32)).astype(jnp.bfloat16)
    grad = dot(high, far_ref[:, :width]) + dot(low, far_ref[:, :width])
    out_ref[:, :width] = (scale * grad).astype(jnp.bfloat16)
    lane = iota((blocks * images, LANES), 1)
    parts = jnp.zeros((blocks * images, LANES), jnp.float32)
    for n in range(3):
        part = loss.astype(jnp.bfloat16).astype(jnp.float32)
        parts = jnp.where(lane == n, part, parts)
        loss = loss - part
    out_ref[:, width:] = parts.astype(jnp.bfloat16)


def grad_kernel(terms_ref, text_ref, loss_ref, grad_ref):
    images, width = text_ref.shape
    terms = terms_ref[...].astype(jnp.float32).reshape(NEAR, images, width + LANES)
    terms = jnp.sum(terms, axis=0)
    loss = jnp.sum(terms[:, width:], axis=-1, keepdims=True)
    diagonal = iota((images, images), 0) == iota((images, images), 1)
    loss_ref[...] = jnp.sum(jnp.where(diagonal, loss, 0.0), axis=0, keepdims=True)
    text = text_ref[...].astype(jnp.float32)
    length = jnp.sqrt(jnp.sum(text * text, axis=-1, keepdims=True) + 1e-06)
    unit = text / length
    grad = terms[:, :width]
    along = jnp.sum(grad * unit, axis=-1, keepdims=True)
    grad_ref[...] = (grad - along * unit) / length


def shards(
    wide, patches, counts, key_weight, value_weight, probe_query, text_embed, labels,
    logit_scale, logit_bias,
):
    images, _, width = patches.shape
    near = [list(range(first, first + NEAR)) for first in range(0, wide, NEAR)]
    far = [list(range(first, wide, NEAR)) for first in range(NEAR)]
    arrays = (text_embed, probe_query, patches, key_weight, value_weight)
    rows = pl.pallas_call(
        pool_kernel,
        out_shape=jax.ShapeDtypeStruct((2 * images, width + LANES), jnp.bfloat16),
        in_specs=[ANY, ANY, ANY, ANY, ANY, SMEM, SMEM],
        out_specs=VMEM,
        scratch_shapes=[pltpu.VMEM(a.shape, a.dtype) for a in arrays]
        + [pltpu.SemaphoreType.DMA((2 * CHUNKS + 3,))],
        compiler_params=pltpu.CompilerParams(vmem_limit_bytes=60 * 2**20),
        name="pool_rows",
    )(*arrays, counts, labels)
    near_rows = lax.all_gather(rows, "wide", axis=0, tiled=True, axis_index_groups=near)
    far_rows = lax.all_gather(rows, "wide", axis=0, tiled=True, axis_index_groups=far)
    terms = pl.pallas_call(
        functools.partial(pair_kernel, images),
        out_shape=jax.ShapeDtypeStruct((NEAR * images, width + LANES), jnp.bfloat16),
        in_specs=[VMEM, VMEM, ANY, ANY],
        out_specs=VMEM,
        scratch_shapes=[
            pltpu.SMEM((1,), jnp.float32),
            pltpu.SMEM((1,), jnp.float32),
            pltpu.SemaphoreType.DMA((2,)),
        ],
        compiler_params=pltpu.CompilerParams(vmem_limit_bytes=32 * 2**20),
        name="pair_terms",
    )(near_rows, far_rows, logit_scale.reshape(1), logit_bias.reshape(1))
    terms = lax.all_to_all(terms, "wide", 0, 0, tiled=True, axis_index_groups=near)
    row_loss, text_grad = pl.pallas_call(
        grad_kernel,
        out_shape=(
            jax.ShapeDtypeStruct((1, images), jnp.float32),
            jax.ShapeDtypeStruct((images, width), jnp.float32),
        ),
        in_specs=[VMEM, VMEM],
        out_specs=(VMEM, VMEM),
        name="text_gradient",
    )(terms, text_embed)
    return (row_loss.reshape(images), text_grad)


def solution(mesh):
    rows = P(("wide", "group"))
    return jax.shard_map(
        functools.partial(shards, mesh.shape["wide"]),
        mesh=mesh,
        in_specs=(rows, rows, P(), P(), P(), rows, rows, P(), P()),
        out_specs=(rows, rows),
        check_vma=False,
    )
```

```python
import functools

import jax
import jax.numpy as jnp
from jax import lax
from jax.experimental import pallas as pl
from jax.experimental.pallas import tpu as pltpu
from jax.sharding import PartitionSpec as P

LANES = 128
CORES = 2
NEAR = 4

VMEM = pl.BlockSpec(memory_space=pltpu.VMEM)
ANY = pl.BlockSpec(memory_space=pl.ANY)


def dot(left, right):
    return jnp.dot(left, right, preferred_element_type=jnp.float32)


def row_dot(left, right):
    return lax.dot_general(
        left, right, (((1,), (1,)), ((), ())), preferred_element_type=jnp.float32
    )


def iota(shape, dim):
    return lax.broadcasted_iota(jnp.int32, shape, dim)


def fetch(sources, targets, sems):
    copies = [
        pltpu.make_async_copy(source, target, sems.at[n])
        for n, (source, target) in enumerate(zip(sources, targets))
    ]
    for copy in copies:
        copy.start()
    return copies


def pool_kernel(*refs):
    inputs, out_ref, scratch = refs[:7], refs[7], refs[8:]
    copies = fetch(inputs, scratch[:7], scratch[7])
    patches_ref, key_ref, value_ref, counts_ref, labels_ref, query_ref, text_ref = scratch[:7]
    patches_copy, key_copy, value_copy = copies[:3]
    images, patch_count, width = patches_ref.shape
    heads, head_size = query_ref.shape
    rows = images * patch_count

    for copy in copies[3:]:
        copy.wait()
    text = text_ref[...].astype(jnp.float32)
    length = jnp.sqrt(jnp.sum(text * text, axis=-1, keepdims=True) + 1e-06)
    out_ref[0:images, 0:width] = (text / length).astype(jnp.bfloat16)
    wide = lax.axis_index("wide")
    lane = iota((images, LANES), 1)
    row = iota((images, LANES), 0)
    place = (lane == wide) | (lane == row + 32)
    out_ref[0:images, width:] = jnp.where(place, 1.0, 0.0).astype(jnp.bfloat16)
    first = jnp.zeros((images, LANES), jnp.int32)
    second = jnp.zeros((images, LANES), jnp.int32)
    valid = jnp.zeros((images, patch_count, heads), jnp.int32)
    image = iota((images, patch_count, heads), 0)
    for i in range(images):
        label = labels_ref[i]
        high = lax.shift_right_logical(label, 4)
        first = jnp.where(row == i, high, first)
        second = jnp.where(row == i, label - 16 * high + 32, second)
        valid = jnp.where(image == i, counts_ref[i], valid)
    place = (lane == first) | (lane == second)
    out_ref[images:, width:] = jnp.where(place, 1.0, 0.0).astype(jnp.bfloat16)
    valid = iota((images, patch_count, heads), 1) < valid

    column = iota((1, width), 1)
    head_of = jnp.zeros((1, width), jnp.int32)
    for h in range(1, heads):
        head_of += (column >= h * head_size).astype(jnp.int32)
    inner = column - head_of * head_size
    spread = jnp.where(iota((head_size, width), 0) == inner, 1.0, 0.0).astype(jnp.bfloat16)
    own = iota((heads, width), 0) == head_of
    query = jnp.where(own, dot(query_ref[...], spread), 0.0).astype(jnp.bfloat16)
    own = jnp.where(own, 1.0, 0.0).astype(jnp.bfloat16)

    patches_copy.wait()
    flat = patches_ref[...].reshape(rows, width)
    key_copy.wait()
    keys = dot(flat, key_ref[...]).astype(jnp.bfloat16)
    scores = row_dot(keys, query)
    value_copy.wait()
    values = dot(flat, value_ref[...]).astype(jnp.bfloat16)
    scores = (scores * (1.0 / head_size**0.5)).reshape(images, patch_count, heads)
    scores = jnp.where(valid, scores, -1e30)
    scores = jnp.exp(scores - jnp.max(scores, axis=1, keepdims=True))
    attend = scores / jnp.sum(scores, axis=1, keepdims=True)
    attend = attend.reshape(rows, heads).astype(jnp.bfloat16)
    terms = dot(attend, own) * values.astype(jnp.float32)
    pooled = jnp.sum(terms.reshape(images, patch_count, width), axis=1)
    pooled = pooled.astype(jnp.bfloat16).astype(jnp.float32)
    length = jnp.sqrt(jnp.sum(pooled * pooled, axis=-1, keepdims=True) + 1e-06)
    out_ref[images:, 0:width] = (pooled / length).astype(jnp.bfloat16)


def pair_kernel(
    images, own_ref, first_ref, second_ref, third_ref, far_ref, scalar_hbm, out_ref,
    scalar_ref, sems,
):
    copy = fetch([scalar_hbm], [scalar_ref], sems)[0]
    near_rows = jnp.concatenate(
        [own_ref[...], first_ref[...], second_ref[...], third_ref[...]], axis=0
    )
    near, width = near_rows.shape[0], near_rows.shape[1] - LANES
    far = far_ref.shape[0]
    raw = row_dot(near_rows[:, :width], far_ref[:, :width])
    match = row_dot(near_rows[:, width:], far_ref[:, width:])
    sign = jnp.where(match > 1.5, 1.0, -1.0)
    copy.wait()
    scale, bias = scalar_ref[0], scalar_ref[1]
    logits = -sign * (scale * raw + bias)
    small = jnp.exp(-jnp.abs(logits))
    softplus = jnp.maximum(logits, 0.0) + jnp.log1p(small)
    slope = -sign * (jnp.where(logits >= 0.0, 1.0, small) / (1.0 + small))
    far_is_text = (iota((near, far), 1) & images) == 0
    loss = jnp.sum(jnp.where(far_is_text, softplus, 0.0), axis=-1, keepdims=True)
    slope = jnp.where(far_is_text, 0.0, slope)
    slope = slope.reshape(NEAR, 2 * images, far)[:, :images].reshape(NEAR * images, far)
    loss = loss.reshape(NEAR, 2 * images, 1)[:, images:].reshape(NEAR * images, 1)
    high = slope.astype(jnp.bfloat16)
    low = (slope - high.astype(jnp.float32)).astype(jnp.bfloat16)
    grad = scale * (dot(high, far_ref[:, :width]) + dot(low, far_ref[:, :width]))
    lane = iota((NEAR * images, LANES), 1)
    parts = jnp.zeros((NEAR * images, LANES), jnp.float32)
    for n in range(3):
        part = loss.astype(jnp.bfloat16).astype(jnp.float32)
        parts = jnp.where(lane == n, part, parts)
        loss = loss - part
    place = own_ref[0:1, width:].astype(jnp.float32).astype(jnp.int32)
    lane = iota((1, LANES), 1)
    place = jnp.sum(jnp.where(lane < 32, place * lane, 0), axis=-1, keepdims=True)
    place = lax.shift_right_logical(place, 1) & (NEAR - 1)
    for target in range(NEAR):
        at = slice(target * images, (target + 1) * images)
        for source, columns in ((grad, slice(0, width)), (parts, slice(width, None))):
            block = source[0:images]
            for n in range(1, NEAR):
                block = jnp.where(place == (target ^ n), source[n * images : (n + 1) * images], block)
            out_ref[at, columns] = block.astype(jnp.bfloat16)


def grad_kernel(terms_ref, text_ref, loss_ref, grad_ref):
    images, width = text_ref.shape
    terms = terms_ref[...].astype(jnp.float32).reshape(NEAR, images, width + LANES)
    terms = jnp.sum(terms, axis=0)
    loss = jnp.sum(terms[:, width:], axis=-1, keepdims=True)
    diagonal = iota((images, images), 0) == iota((images, images), 1)
    loss_ref[...] = jnp.sum(jnp.where(diagonal, loss, 0.0), axis=0, keepdims=True)
    text = text_ref[...].astype(jnp.float32)
    length = jnp.sqrt(jnp.sum(text * text, axis=-1, keepdims=True) + 1e-06)
    unit = text / length
    grad = terms[:, :width]
    along = jnp.sum(grad * unit, axis=-1, keepdims=True)
    grad_ref[...] = (grad - along * unit) / length


def shards(
    wide, patches, counts, key_weight, value_weight, probe_query, text_embed, labels,
    logit_scale, logit_bias,
):
    images, _, width = patches.shape
    block = NEAR * CORES
    near = [
        [first + core + CORES * chip for chip in range(NEAR)]
        for first in range(0, wide, block)
        for core in range(CORES)
    ]
    far = [
        [first + CORES * chip + core for first in range(0, wide, block) for core in range(CORES)]
        for chip in range(NEAR)
    ]
    arrays = (patches, key_weight, value_weight, counts, labels, probe_query, text_embed)
    places = (pltpu.VMEM,) * 3 + (pltpu.SMEM,) * 2 + (pltpu.VMEM,) * 2
    rows = pl.pallas_call(
        pool_kernel,
        out_shape=jax.ShapeDtypeStruct((2 * images, width + LANES), jnp.bfloat16),
        in_specs=[ANY] * 7,
        out_specs=VMEM,
        scratch_shapes=[place(a.shape, a.dtype) for place, a in zip(places, arrays)]
        + [pltpu.SemaphoreType.DMA((7,))],
        compiler_params=pltpu.CompilerParams(vmem_limit_bytes=60 * 2**20),
        name="pool_rows",
    )(*arrays)
    near_rows = [
        lax.ppermute(rows, "wide", [(i, i ^ (CORES * n)) for i in range(wide)])
        for n in range(1, NEAR)
    ]
    far_rows = lax.all_gather(rows, "wide", axis=0, tiled=True, axis_index_groups=far)
    terms = pl.pallas_call(
        functools.partial(pair_kernel, images),
        out_shape=jax.ShapeDtypeStruct((NEAR * images, width + LANES), jnp.bfloat16),
        in_specs=[VMEM] * 5 + [ANY],
        out_specs=VMEM,
        scratch_shapes=[pltpu.SMEM((2,), jnp.float32), pltpu.SemaphoreType.DMA((1,))],
        compiler_params=pltpu.CompilerParams(vmem_limit_bytes=32 * 2**20),
        name="pair_terms",
    )(rows, *near_rows, far_rows, jnp.stack([logit_scale, logit_bias]))
    terms = lax.all_to_all(terms, "wide", 0, 0, tiled=True, axis_index_groups=near)
    row_loss, text_grad = pl.pallas_call(
        grad_kernel,
        out_shape=(
            jax.ShapeDtypeStruct((1, images), jnp.float32),
            jax.ShapeDtypeStruct((images, width), jnp.float32),
        ),
        in_specs=[VMEM, VMEM],
        out_specs=(VMEM, VMEM),
        name="text_gradient",
    )(terms, text_embed)
    return (row_loss.reshape(images), text_grad)


def solution(mesh):
    rows = P(("wide", "group"))
    return jax.shard_map(
        functools.partial(shards, mesh.shape["wide"]),
        mesh=mesh,
        in_specs=(rows, rows, P(), P(), P(), rows, rows, P(), P()),
        out_specs=(rows, rows),
        check_vma=False,
    )
```

```python
import functools

import jax
import jax.numpy as jnp
from jax import lax
from jax.experimental import pallas as pl
from jax.experimental.pallas import tpu as pltpu
from jax.sharding import PartitionSpec as P

LANES = 128
CORES = 2
NEAR = 4

VMEM = pl.BlockSpec(memory_space=pltpu.VMEM)
SMEM = pl.BlockSpec(memory_space=pltpu.SMEM)
ANY = pl.BlockSpec(memory_space=pl.ANY)


def dot(left, right):
    return jnp.dot(left, right, preferred_element_type=jnp.float32)


def row_dot(left, right):
    return lax.dot_general(
        left, right, (((1,), (1,)), ((), ())), preferred_element_type=jnp.float32
    )


def iota(shape, dim):
    return lax.broadcasted_iota(jnp.int32, shape, dim)


def start(copies):
    for copy in copies:
        copy.start()


def wait(copies):
    for copy in copies:
        copy.wait()


def pool_kernel(*refs):
    inputs, out_ref, scratch = refs[:7], refs[7], refs[8:]
    patches_ref, key_ref, value_ref, counts_ref, labels_ref, query_ref, text_ref = scratch[:7]
    sems = scratch[7]
    images, patch_count, width = patches_ref.shape
    heads, head_size = query_ref.shape
    rows = images * patch_count
    copies = [
        pltpu.make_async_copy(source, target, sems.at[n])
        for n, (source, target) in enumerate(zip(inputs, scratch[:7]))
    ]
    patches_copy, value_copy, small_copies = copies[0], copies[2], copies[3:]
    cut = width // (2 * LANES) * LANES + LANES
    key_parts = [slice(0, cut), slice(cut, width)]
    key_copies = [
        pltpu.make_async_copy(inputs[1].at[:, at], key_ref.at[:, at], sems.at[n])
        for n, at in zip((1, 7), key_parts)
    ]
    start(small_copies + [patches_copy] + key_copies)
    wait(small_copies)
    value_copy.start()
    text = text_ref[...].astype(jnp.float32)
    length = jnp.sqrt(jnp.sum(text * text, axis=-1, keepdims=True) + 1e-06)
    out_ref[0:images, 0:width] = (text / length).astype(jnp.bfloat16)
    wide = lax.axis_index("wide")
    lane = iota((images, LANES), 1)
    row = iota((images, LANES), 0)
    place = (lane == wide) | (lane == row + 32)
    out_ref[0:images, width:] = jnp.where(place, 1.0, 0.0).astype(jnp.bfloat16)
    first = jnp.zeros((images, LANES), jnp.int32)
    second = jnp.zeros((images, LANES), jnp.int32)
    valid = jnp.zeros((images, patch_count, heads), jnp.int32)
    image = iota((images, patch_count, heads), 0)
    for i in range(images):
        label = labels_ref[i]
        high = lax.shift_right_logical(label, 4)
        first = jnp.where(row == i, high, first)
        second = jnp.where(row == i, label - 16 * high + 32, second)
        valid = jnp.where(image == i, counts_ref[i], valid)
    place = (lane == first) | (lane == second)
    out_ref[images:, width:] = jnp.where(place, 1.0, 0.0).astype(jnp.bfloat16)
    valid = iota((images, patch_count, heads), 1) < valid

    column = iota((1, width), 1)
    head_of = jnp.zeros((1, width), jnp.int32)
    for h in range(1, heads):
        head_of += (column >= h * head_size).astype(jnp.int32)
    inner = column - head_of * head_size
    spread = jnp.where(iota((head_size, width), 0) == inner, 1.0, 0.0).astype(jnp.bfloat16)
    own = iota((heads, width), 0) == head_of
    query = jnp.where(own, dot(query_ref[...], spread), 0.0).astype(jnp.bfloat16)
    own = jnp.where(own, 1.0, 0.0).astype(jnp.bfloat16)

    patches_copy.wait()
    flat = patches_ref[...].reshape(rows, width)
    scores = jnp.zeros((rows, heads), jnp.float32)
    for at, copy in zip(key_parts, key_copies):
        copy.wait()
        keys = dot(flat, key_ref[:, at]).astype(jnp.bfloat16)
        scores += row_dot(keys, query[:, at])
    value_copy.wait()
    values = dot(flat, value_ref[...]).astype(jnp.bfloat16)
    scores = (scores * (1.0 / head_size**0.5)).reshape(images, patch_count, heads)
    scores = jnp.where(valid, scores, -1e30)
    scores = jnp.exp(scores - jnp.max(scores, axis=1, keepdims=True))
    attend = scores / jnp.sum(scores, axis=1, keepdims=True)
    attend = attend.reshape(rows, heads).astype(jnp.bfloat16)
    terms = dot(attend, own) * values.astype(jnp.float32)
    pooled = jnp.sum(terms.reshape(images, patch_count, width), axis=1)
    pooled = pooled.astype(jnp.bfloat16).astype(jnp.float32)
    length = jnp.sqrt(jnp.sum(pooled * pooled, axis=-1, keepdims=True) + 1e-06)
    out_ref[images:, 0:width] = (pooled / length).astype(jnp.bfloat16)


def pair_kernel(
    images, pair_ref, other_ref, far_ref, scale_ref, bias_ref, out_ref
):
    near_rows = jnp.concatenate([pair_ref[...], other_ref[...]], axis=0)
    near, width = near_rows.shape[0], near_rows.shape[1] - LANES
    far = far_ref.shape[0]
    raw = row_dot(near_rows[:, :width], far_ref[:, :width])
    match = row_dot(near_rows[:, width:], far_ref[:, width:])
    sign = jnp.where(match > 1.5, 1.0, -1.0)
    scale, bias = scale_ref[0], bias_ref[0]
    logits = -sign * (scale * raw + bias)
    small = jnp.exp(-jnp.abs(logits))
    softplus = jnp.maximum(logits, 0.0) + jnp.log1p(small)
    slope = -sign * (jnp.where(logits >= 0.0, 1.0, small) / (1.0 + small))
    far_is_text = (iota((near, far), 1) & images) == 0
    loss = jnp.sum(jnp.where(far_is_text, softplus, 0.0), axis=-1, keepdims=True)
    slope = jnp.where(far_is_text, 0.0, slope)
    slope = slope.reshape(NEAR, 2 * images, far)[:, :images].reshape(NEAR * images, far)
    loss = loss.reshape(NEAR, 2 * images, 1)[:, images:].reshape(NEAR * images, 1)
    high = slope.astype(jnp.bfloat16)
    low = (slope - high.astype(jnp.float32)).astype(jnp.bfloat16)
    grad = scale * (dot(high, far_ref[:, :width]) + dot(low, far_ref[:, :width]))
    lane = iota((NEAR * images, LANES), 1)
    parts = jnp.zeros((NEAR * images, LANES), jnp.float32)
    for n in range(3):
        part = loss.astype(jnp.bfloat16).astype(jnp.float32)
        parts = jnp.where(lane == n, part, parts)
        loss = loss - part
    place = pair_ref[0:1, width:].astype(jnp.float32).astype(jnp.int32)
    lane = iota((1, LANES), 1)
    place = jnp.sum(jnp.where(lane < 32, place * lane, 0), axis=-1, keepdims=True)
    second = (place & (CORES * NEAR // 2)) != 0
    half = NEAR // 2 * images
    for source, columns in ((grad, slice(0, width)), (parts, slice(width, None))):
        low, high = source[:half], source[half:]
        out_ref[:half, columns] = jnp.where(second, high, low).astype(jnp.bfloat16)
        out_ref[half:, columns] = jnp.where(second, low, high).astype(jnp.bfloat16)


def grad_kernel(terms_ref, text_ref, loss_ref, grad_ref):
    images, width = text_ref.shape
    terms = terms_ref[...].astype(jnp.float32).reshape(NEAR, images, width + LANES)
    terms = jnp.sum(terms, axis=0)
    loss = jnp.sum(terms[:, width:], axis=-1, keepdims=True)
    diagonal = iota((images, images), 0) == iota((images, images), 1)
    loss_ref[...] = jnp.sum(jnp.where(diagonal, loss, 0.0), axis=0, keepdims=True)
    text = text_ref[...].astype(jnp.float32)
    length = jnp.sqrt(jnp.sum(text * text, axis=-1, keepdims=True) + 1e-06)
    unit = text / length
    grad = terms[:, :width]
    along = jnp.sum(grad * unit, axis=-1, keepdims=True)
    grad_ref[...] = (grad - along * unit) / length


def shards(
    wide, patches, counts, key_weight, value_weight, probe_query, text_embed, labels,
    logit_scale, logit_bias,
):
    images, _, width = patches.shape
    block = NEAR * CORES
    near = [
        [first + core + CORES * chip for chip in range(NEAR)]
        for first in range(0, wide, block)
        for core in range(CORES)
    ]
    pairs = [
        [first + core, first + CORES + core]
        for first in range(0, wide, 2 * CORES)
        for core in range(CORES)
    ]
    far = [
        [first + CORES * chip + core for first in range(0, wide, block) for core in range(CORES)]
        for chip in range(NEAR)
    ]
    arrays = (patches, key_weight, value_weight, counts, labels, probe_query, text_embed)
    places = (pltpu.VMEM,) * 3 + (pltpu.SMEM,) * 2 + (pltpu.VMEM,) * 2
    rows = pl.pallas_call(
        pool_kernel,
        out_shape=jax.ShapeDtypeStruct((2 * images, width + LANES), jnp.bfloat16),
        in_specs=[ANY] * 7,
        out_specs=VMEM,
        scratch_shapes=[place(a.shape, a.dtype) for place, a in zip(places, arrays)]
        + [pltpu.SemaphoreType.DMA((8,))],
        compiler_params=pltpu.CompilerParams(vmem_limit_bytes=60 * 2**20),
        name="pool_rows",
    )(*arrays)
    pair_rows = lax.all_gather(rows, "wide", axis=0, tiled=True, axis_index_groups=pairs)
    other_rows = lax.ppermute(pair_rows, "wide", [(i, i ^ block // 2) for i in range(wide)])
    far_rows = lax.all_gather(rows, "wide", axis=0, tiled=True, axis_index_groups=far)
    terms = pl.pallas_call(
        functools.partial(pair_kernel, images),
        out_shape=jax.ShapeDtypeStruct((NEAR * images, width + LANES), jnp.bfloat16),
        in_specs=[VMEM] * 3 + [SMEM] * 2,
        out_specs=VMEM,
        compiler_params=pltpu.CompilerParams(vmem_limit_bytes=32 * 2**20),
        name="pair_terms",
    )(pair_rows, other_rows, far_rows, logit_scale.reshape(1), logit_bias.reshape(1))
    terms = lax.all_to_all(terms, "wide", 0, 0, tiled=True, axis_index_groups=near)
    row_loss, text_grad = pl.pallas_call(
        grad_kernel,
        out_shape=(
            jax.ShapeDtypeStruct((1, images), jnp.float32),
            jax.ShapeDtypeStruct((images, width), jnp.float32),
        ),
        in_specs=[VMEM, VMEM],
        out_specs=(VMEM, VMEM),
        name="text_gradient",
    )(terms, text_embed)
    return (row_loss.reshape(images), text_grad)


def solution(mesh):
    rows = P(("wide", "group"))
    return jax.shard_map(
        functools.partial(shards, mesh.shape["wide"]),
        mesh=mesh,
        in_specs=(rows, rows, P(), P(), P(), rows, rows, P(), P()),
        out_specs=(rows, rows),
        check_vma=False,
    )
```

```python
import functools

import jax
import jax.numpy as jnp
from jax import lax
from jax.experimental import pallas as pl
from jax.experimental.pallas import tpu as pltpu
from jax.sharding import PartitionSpec as P

LANES = 128
CORES = 2
NEAR = 4

VMEM = pl.BlockSpec(memory_space=pltpu.VMEM)
SMEM = pl.BlockSpec(memory_space=pltpu.SMEM)
ANY = pl.BlockSpec(memory_space=pl.ANY)


def dot(left, right):
    return jnp.dot(left, right, preferred_element_type=jnp.float32)


def row_dot(left, right):
    return lax.dot_general(
        left, right, (((1,), (1,)), ((), ())), preferred_element_type=jnp.float32
    )


def iota(shape, dim):
    return lax.broadcasted_iota(jnp.int32, shape, dim)


def start(copies):
    for copy in copies:
        copy.start()


def wait(copies):
    for copy in copies:
        copy.wait()


def pool_kernel(*refs):
    inputs, out_ref, scratch = refs[:7], refs[7], refs[8:]
    patches_ref, key_ref, value_ref, counts_ref, labels_ref, query_ref, text_ref = scratch[:7]
    sems = scratch[7]
    images, patch_count, width = patches_ref.shape
    heads, head_size = query_ref.shape
    rows = images * patch_count
    patches_copy, value_copy, *small_copies = [
        pltpu.make_async_copy(inputs[n], scratch[n], sems.at[n]) for n in (0, 2, 3, 4, 5, 6)
    ]
    cut = width // (2 * LANES) * LANES + LANES
    key_parts = [slice(0, cut), slice(cut, width)]
    key_copies = [
        pltpu.make_async_copy(inputs[1].at[:, at], key_ref.at[:, at], sems.at[n])
        for n, at in zip((1, 7), key_parts)
    ]
    start(small_copies + [patches_copy] + key_copies)
    wait(small_copies)
    value_copy.start()
    text = text_ref[...].astype(jnp.float32)
    length = jnp.sqrt(jnp.sum(text * text, axis=-1, keepdims=True) + 1e-06)
    out_ref[0:images, 0:width] = (text / length).astype(jnp.bfloat16)
    wide = lax.axis_index("wide")
    lane = iota((images, LANES), 1)
    row = iota((images, LANES), 0)
    place = (lane == wide) | (lane == row + 32)
    out_ref[0:images, width:] = jnp.where(place, 1.0, 0.0).astype(jnp.bfloat16)
    first = jnp.zeros((images, LANES), jnp.int32)
    second = jnp.zeros((images, LANES), jnp.int32)
    valid = jnp.zeros((images, patch_count, heads), jnp.int32)
    image = iota((images, patch_count, heads), 0)
    for i in range(images):
        label = labels_ref[i]
        high = lax.shift_right_logical(label, 4)
        first = jnp.where(row == i, high, first)
        second = jnp.where(row == i, label - 16 * high + 32, second)
        valid = jnp.where(image == i, counts_ref[i], valid)
    place = (lane == first) | (lane == second)
    out_ref[images:, width:] = jnp.where(place, 1.0, 0.0).astype(jnp.bfloat16)
    valid = iota((images, patch_count, heads), 1) < valid

    column = iota((1, width), 1)
    head_of = jnp.zeros((1, width), jnp.int32)
    for h in range(1, heads):
        head_of += (column >= h * head_size).astype(jnp.int32)
    inner = column - head_of * head_size
    spread = jnp.where(iota((head_size, width), 0) == inner, 1.0, 0.0).astype(jnp.bfloat16)
    own = iota((heads, width), 0) == head_of
    query = jnp.where(own, dot(query_ref[...], spread), 0.0).astype(jnp.bfloat16)
    own = jnp.where(own, 1.0, 0.0).astype(jnp.bfloat16)

    patches_copy.wait()
    flat = patches_ref[...].reshape(rows, width)
    scores = jnp.zeros((rows, heads), jnp.float32)
    for at, copy in zip(key_parts, key_copies):
        copy.wait()
        keys = dot(flat, key_ref[:, at]).astype(jnp.bfloat16)
        scores += row_dot(keys, query[:, at])
    value_copy.wait()
    values = dot(flat, value_ref[...]).astype(jnp.bfloat16)
    scores = (scores * (1.0 / head_size**0.5)).reshape(images, patch_count, heads)
    scores = jnp.where(valid, scores, -1e30)
    scores = jnp.exp(scores - jnp.max(scores, axis=1, keepdims=True))
    attend = scores / jnp.sum(scores, axis=1, keepdims=True)
    attend = attend.reshape(rows, heads).astype(jnp.bfloat16)
    terms = dot(attend, own) * values.astype(jnp.float32)
    pooled = jnp.sum(terms.reshape(images, patch_count, width), axis=1)
    pooled = pooled.astype(jnp.bfloat16).astype(jnp.float32)
    length = jnp.sqrt(jnp.sum(pooled * pooled, axis=-1, keepdims=True) + 1e-06)
    out_ref[images:, 0:width] = (pooled / length).astype(jnp.bfloat16)


def pair_kernel(images, own_ref, other_ref, scale_ref, bias_ref, out_ref):
    core = lax.axis_index("wide") & 1
    scale, bias = scale_ref[0], bias_ref[0]
    for this, (near_ref, far_ref) in enumerate(((own_ref, other_ref), (other_ref, own_ref))):
        pl.when(core == this)(
            functools.partial(
                pair_terms, images, this, near_ref, far_ref, scale, bias, out_ref
            )
        )


def pair_terms(images, core, near_ref, far_ref, scale, bias, out_ref):
    rows = 2 * images
    near_rows = jnp.concatenate(
        [near_ref[pl.ds((CORES * n + core) * rows, rows)] for n in range(NEAR)]
    )
    near, width = near_rows.shape[0], near_rows.shape[1] - LANES
    far = far_ref.shape[0]
    raw = row_dot(near_rows[:, :width], far_ref[:, :width])
    match = row_dot(near_rows[:, width:], far_ref[:, width:])
    sign = jnp.where(match > 1.5, 1.0, -1.0)
    logits = -sign * (scale * raw + bias)
    small = jnp.exp(-jnp.abs(logits))
    softplus = jnp.maximum(logits, 0.0) + jnp.log1p(small)
    slope = -sign * (jnp.where(logits >= 0.0, 1.0, small) / (1.0 + small))
    far_is_text = (iota((near, far), 1) & images) == 0
    loss = jnp.sum(jnp.where(far_is_text, softplus, 0.0), axis=-1, keepdims=True)
    slope = jnp.where(far_is_text, 0.0, slope)
    slope = slope.reshape(NEAR, 2 * images, far)[:, :images].reshape(NEAR * images, far)
    loss = loss.reshape(NEAR, 2 * images, 1)[:, images:].reshape(NEAR * images, 1)
    high = slope.astype(jnp.bfloat16)
    low = (slope - high.astype(jnp.float32)).astype(jnp.bfloat16)
    grad = scale * (dot(high, far_ref[:, :width]) + dot(low, far_ref[:, :width]))
    lane = iota((NEAR * images, LANES), 1)
    parts = jnp.zeros((NEAR * images, LANES), jnp.float32)
    for n in range(3):
        part = loss.astype(jnp.bfloat16).astype(jnp.float32)
        parts = jnp.where(lane == n, part, parts)
        loss = loss - part
    out_ref[:, :width] = grad.astype(jnp.bfloat16)
    out_ref[:, width:] = parts.astype(jnp.bfloat16)


def grad_kernel(terms_ref, text_ref, loss_ref, grad_ref):
    images, width = text_ref.shape
    terms = terms_ref[...].astype(jnp.float32).reshape(NEAR, images, width + LANES)
    terms = jnp.sum(terms, axis=0)
    loss = jnp.sum(terms[:, width:], axis=-1, keepdims=True)
    diagonal = iota((images, images), 0) == iota((images, images), 1)
    loss_ref[...] = jnp.sum(jnp.where(diagonal, loss, 0.0), axis=0, keepdims=True)
    text = text_ref[...].astype(jnp.float32)
    length = jnp.sqrt(jnp.sum(text * text, axis=-1, keepdims=True) + 1e-06)
    unit = text / length
    grad = terms[:, :width]
    along = jnp.sum(grad * unit, axis=-1, keepdims=True)
    grad_ref[...] = (grad - along * unit) / length


def shards(
    wide, patches, counts, key_weight, value_weight, probe_query, text_embed, labels,
    logit_scale, logit_bias,
):
    images, _, width = patches.shape
    block = NEAR * CORES
    near = [
        [first + core + CORES * chip for chip in range(NEAR)]
        for first in range(0, wide, block)
        for core in range(CORES)
    ]
    cores = [[first, first + 1] for first in range(0, wide, CORES)]
    far = [
        [first + CORES * chip + 1 for first in range(0, wide, block)] for chip in range(NEAR)
    ]
    mixed = near[::CORES] + far
    arrays = (patches, key_weight, value_weight, counts, labels, probe_query, text_embed)
    places = (pltpu.VMEM,) * 3 + (pltpu.SMEM,) * 2 + (pltpu.VMEM,) * 2
    rows = pl.pallas_call(
        pool_kernel,
        out_shape=jax.ShapeDtypeStruct((2 * images, width + LANES), jnp.bfloat16),
        in_specs=[ANY] * 7,
        out_specs=VMEM,
        scratch_shapes=[place(a.shape, a.dtype) for place, a in zip(places, arrays)]
        + [pltpu.SemaphoreType.DMA((8,))],
        compiler_params=pltpu.CompilerParams(vmem_limit_bytes=60 * 2**20),
        name="pool_rows",
    )(*arrays)
    rows = lax.all_gather(rows, "wide", axis=0, tiled=True, axis_index_groups=cores)
    rows = lax.all_gather(rows, "wide", axis=0, tiled=True, axis_index_groups=mixed)
    other_rows = lax.ppermute(rows, "wide", [(i, i ^ 1) for i in range(wide)])
    terms = pl.pallas_call(
        functools.partial(pair_kernel, images),
        out_shape=jax.ShapeDtypeStruct((NEAR * images, width + LANES), jnp.bfloat16),
        in_specs=[VMEM] * 2 + [SMEM] * 2,
        out_specs=VMEM,
        compiler_params=pltpu.CompilerParams(vmem_limit_bytes=32 * 2**20),
        name="pair_terms",
    )(rows, other_rows, logit_scale.reshape(1), logit_bias.reshape(1))
    terms = lax.all_to_all(terms, "wide", 0, 0, tiled=True, axis_index_groups=near)
    row_loss, text_grad = pl.pallas_call(
        grad_kernel,
        out_shape=(
            jax.ShapeDtypeStruct((1, images), jnp.float32),
            jax.ShapeDtypeStruct((images, width), jnp.float32),
        ),
        in_specs=[VMEM, VMEM],
        out_specs=(VMEM, VMEM),
        name="text_gradient",
    )(terms, text_embed)
    return (row_loss.reshape(images), text_grad)


def solution(mesh):
    rows = P(("wide", "group"))
    return jax.shard_map(
        functools.partial(shards, mesh.shape["wide"]),
        mesh=mesh,
        in_specs=(rows, rows, P(), P(), P(), rows, rows, P(), P()),
        out_specs=(rows, rows),
        check_vma=False,
    )
```

```python
import functools

import jax
import jax.numpy as jnp
from jax import lax
from jax.experimental import pallas as pl
from jax.experimental.pallas import tpu as pltpu
from jax.sharding import PartitionSpec as P

LANES = 128
CORES = 2
NEAR = 4

VMEM = pl.BlockSpec(memory_space=pltpu.VMEM)
SMEM = pl.BlockSpec(memory_space=pltpu.SMEM)
ANY = pl.BlockSpec(memory_space=pl.ANY)


def dot(left, right):
    return jnp.dot(left, right, preferred_element_type=jnp.float32)


def row_dot(left, right):
    return lax.dot_general(
        left, right, (((1,), (1,)), ((), ())), preferred_element_type=jnp.float32
    )


def iota(shape, dim):
    return lax.broadcasted_iota(jnp.int32, shape, dim)


def start(copies):
    for copy in copies:
        copy.start()


def wait(copies):
    for copy in copies:
        copy.wait()


def put_rows(ref, first, rows):
    images, width = rows.shape
    for n in range(width // LANES):
        at = 2 * images * n + first
        ref[at : at + images] = rows[:, n * LANES : (n + 1) * LANES]


def get_rows(ref, first, images, width):
    step = 2 * images
    return jnp.concatenate(
        [ref[first + step * n : first + step * (n + 1)] for n in range(width // LANES)], axis=1
    )


def get_marks(ref, first, images, width, wide):
    row, lane = iota((images, LANES), 0), iota((images, LANES), 1)
    texts = jnp.where((lane == wide) | (lane == row + 32), 1.0, 0.0).astype(jnp.bfloat16)
    first += 2 * images * width // LANES
    return [texts, ref[first : first + images]]


def pool_kernel(*refs):
    inputs, out_ref, scratch = refs[:7], refs[7], refs[8:]
    patches_ref, key_ref, value_ref, counts_ref, labels_ref, query_ref, text_ref = scratch[:7]
    sems = scratch[7]
    images, patch_count, width = patches_ref.shape
    heads, head_size = query_ref.shape
    rows = images * patch_count
    patches_copy, value_copy, *small_copies = [
        pltpu.make_async_copy(inputs[n], scratch[n], sems.at[n]) for n in (0, 2, 3, 4, 5, 6)
    ]
    cut = width // (2 * LANES) * LANES + LANES
    key_parts = [slice(0, cut), slice(cut, width)]
    key_copies = [
        pltpu.make_async_copy(inputs[1].at[:, at], key_ref.at[:, at], sems.at[n])
        for n, at in zip((1, 7), key_parts)
    ]
    start(small_copies + [patches_copy] + key_copies)
    wait(small_copies)
    value_copy.start()
    text = text_ref[...].astype(jnp.float32)
    length = jnp.sqrt(jnp.sum(text * text, axis=-1, keepdims=True) + 1e-06)
    put_rows(out_ref, 0, (text / length).astype(jnp.bfloat16))
    lane = iota((images, LANES), 1)
    row = iota((images, LANES), 0)
    first = jnp.zeros((images, LANES), jnp.int32)
    second = jnp.zeros((images, LANES), jnp.int32)
    valid = jnp.zeros((images, patch_count, heads), jnp.int32)
    image = iota((images, patch_count, heads), 0)
    for i in range(images):
        label = labels_ref[i]
        high = lax.shift_right_logical(label, 4)
        first = jnp.where(row == i, high, first)
        second = jnp.where(row == i, label - 16 * high + 32, second)
        valid = jnp.where(image == i, counts_ref[i], valid)
    place = (lane == first) | (lane == second)
    out_ref[2 * images * width // LANES :] = jnp.where(place, 1.0, 0.0).astype(jnp.bfloat16)
    valid = iota((images, patch_count, heads), 1) < valid

    column = iota((1, width), 1)
    head_of = jnp.zeros((1, width), jnp.int32)
    for h in range(1, heads):
        head_of += (column >= h * head_size).astype(jnp.int32)
    inner = column - head_of * head_size
    spread = jnp.where(iota((head_size, width), 0) == inner, 1.0, 0.0).astype(jnp.bfloat16)
    own = iota((heads, width), 0) == head_of
    query = jnp.where(own, dot(query_ref[...], spread), 0.0).astype(jnp.bfloat16)
    own = jnp.where(own, 1.0, 0.0).astype(jnp.bfloat16)

    patches_copy.wait()
    flat = patches_ref[...].reshape(rows, width)
    scores = jnp.zeros((rows, heads), jnp.float32)
    for at, copy in zip(key_parts, key_copies):
        copy.wait()
        keys = dot(flat, key_ref[:, at]).astype(jnp.bfloat16)
        scores += row_dot(keys, query[:, at])
    value_copy.wait()
    values = dot(flat, value_ref[...]).astype(jnp.bfloat16)
    scores = (scores * (1.0 / head_size**0.5)).reshape(images, patch_count, heads)
    scores = jnp.where(valid, scores, -1e30)
    scores = jnp.exp(scores - jnp.max(scores, axis=1, keepdims=True))
    attend = scores / jnp.sum(scores, axis=1, keepdims=True)
    attend = attend.reshape(rows, heads).astype(jnp.bfloat16)
    terms = dot(attend, own) * values.astype(jnp.float32)
    pooled = jnp.sum(terms.reshape(images, patch_count, width), axis=1)
    pooled = pooled.astype(jnp.bfloat16).astype(jnp.float32)
    length = jnp.sqrt(jnp.sum(pooled * pooled, axis=-1, keepdims=True) + 1e-06)
    put_rows(out_ref, images, (pooled / length).astype(jnp.bfloat16))


def pair_kernel(images, width, own_ref, other_ref, scale_ref, bias_ref, out_ref):
    wide = lax.axis_index("wide")
    core = wide & (CORES - 1)
    scale, bias = scale_ref[0], bias_ref[0]
    for this, (near_ref, far_ref) in enumerate(((own_ref, other_ref), (other_ref, own_ref))):
        pl.when(core == this)(
            functools.partial(
                pair_terms, images, width, wide, this, near_ref, far_ref, scale, bias, out_ref
            )
        )


def pair_terms(images, width, wide, core, near_ref, far_ref, scale, bias, out_ref):
    size = 2 * images * width // LANES + images
    block = CORES * NEAR
    near_blocks = [
        (near_ref, (CORES * n + core) * size, (wide & ~(block - 1)) + CORES * n + core)
        for n in range(NEAR)
    ]
    far_blocks = [
        (far_ref, n * size, (wide & (block - CORES)) + n // CORES * block + n % CORES)
        for n in range(far_ref.shape[0] // size)
    ]
    near_rows, far_rows = (
        jnp.concatenate([get_rows(ref, at, images, width) for ref, at, _ in blocks])
        for blocks in (near_blocks, far_blocks)
    )
    near_marks, far_marks = (
        jnp.concatenate(sum((get_marks(ref, at, images, width, w) for ref, at, w in blocks), []))
        for blocks in (near_blocks, far_blocks)
    )
    near, far = near_rows.shape[0], far_rows.shape[0]
    raw = row_dot(near_rows, far_rows)
    match = row_dot(near_marks, far_marks)
    sign = jnp.where(match > 1.5, 1.0, -1.0)
    logits = -sign * (scale * raw + bias)
    small = jnp.exp(-jnp.abs(logits))
    softplus = jnp.maximum(logits, 0.0) + jnp.log1p(small)
    slope = -sign * (jnp.where(logits >= 0.0, 1.0, small) / (1.0 + small))
    far_is_text = (iota((near, far), 1) & images) == 0
    loss = jnp.sum(jnp.where(far_is_text, softplus, 0.0), axis=-1, keepdims=True)
    slope = jnp.where(far_is_text, 0.0, slope)
    slope = slope.reshape(NEAR, 2 * images, far)[:, :images].reshape(NEAR * images, far)
    loss = loss.reshape(NEAR, 2 * images, 1)[:, images:].reshape(NEAR * images, 1)
    high = slope.astype(jnp.bfloat16)
    low = (slope - high.astype(jnp.float32)).astype(jnp.bfloat16)
    grad = scale * (dot(high, far_rows) + dot(low, far_rows))
    lane = iota((NEAR * images, LANES), 1)
    parts = jnp.zeros((NEAR * images, LANES), jnp.float32)
    for n in range(3):
        part = loss.astype(jnp.bfloat16).astype(jnp.float32)
        parts = jnp.where(lane == n, part, parts)
        loss = loss - part
    out_ref[:, :width] = grad.astype(jnp.bfloat16)
    out_ref[:, width:] = parts.astype(jnp.bfloat16)


def grad_kernel(terms_ref, text_ref, loss_ref, grad_ref):
    images, width = text_ref.shape
    terms = terms_ref[...].astype(jnp.float32).reshape(NEAR, images, width + LANES)
    terms = jnp.sum(terms, axis=0)
    loss = jnp.sum(terms[:, width:], axis=-1, keepdims=True)
    diagonal = iota((images, images), 0) == iota((images, images), 1)
    loss_ref[...] = jnp.sum(jnp.where(diagonal, loss, 0.0), axis=0, keepdims=True)
    text = text_ref[...].astype(jnp.float32)
    length = jnp.sqrt(jnp.sum(text * text, axis=-1, keepdims=True) + 1e-06)
    unit = text / length
    grad = terms[:, :width]
    along = jnp.sum(grad * unit, axis=-1, keepdims=True)
    grad_ref[...] = (grad - along * unit) / length


def shards(
    wide, patches, counts, key_weight, value_weight, probe_query, text_embed, labels,
    logit_scale, logit_bias,
):
    images, _, width = patches.shape
    block = NEAR * CORES
    near = [
        [first + core + CORES * chip for chip in range(NEAR)]
        for first in range(0, wide, block)
        for core in range(CORES)
    ]
    cores = [[first, first + 1] for first in range(0, wide, CORES)]
    far = [
        [first + CORES * chip + 1 for first in range(0, wide, block)] for chip in range(NEAR)
    ]
    mixed = near[::CORES] + far
    arrays = (patches, key_weight, value_weight, counts, labels, probe_query, text_embed)
    places = (pltpu.VMEM,) * 3 + (pltpu.SMEM,) * 2 + (pltpu.VMEM,) * 2
    rows = pl.pallas_call(
        pool_kernel,
        out_shape=jax.ShapeDtypeStruct(
            (2 * images * width // LANES + images, LANES), jnp.bfloat16
        ),
        in_specs=[ANY] * 7,
        out_specs=VMEM,
        scratch_shapes=[place(a.shape, a.dtype) for place, a in zip(places, arrays)]
        + [pltpu.SemaphoreType.DMA((8,))],
        compiler_params=pltpu.CompilerParams(vmem_limit_bytes=60 * 2**20),
        name="pool_rows",
    )(*arrays)
    rows = lax.all_gather(rows, "wide", axis=0, tiled=True, axis_index_groups=cores)
    rows = lax.all_gather(rows, "wide", axis=0, tiled=True, axis_index_groups=mixed)
    other_rows = lax.ppermute(rows, "wide", [(i, i ^ 1) for i in range(wide)])
    terms = pl.pallas_call(
        functools.partial(pair_kernel, images, width),
        out_shape=jax.ShapeDtypeStruct((NEAR * images, width + LANES), jnp.bfloat16),
        in_specs=[VMEM] * 2 + [SMEM] * 2,
        out_specs=VMEM,
        compiler_params=pltpu.CompilerParams(vmem_limit_bytes=32 * 2**20),
        name="pair_terms",
    )(rows, other_rows, logit_scale.reshape(1), logit_bias.reshape(1))
    terms = lax.all_to_all(terms, "wide", 0, 0, tiled=True, axis_index_groups=near)
    row_loss, text_grad = pl.pallas_call(
        grad_kernel,
        out_shape=(
            jax.ShapeDtypeStruct((1, images), jnp.float32),
            jax.ShapeDtypeStruct((images, width), jnp.float32),
        ),
        in_specs=[VMEM, VMEM],
        out_specs=(VMEM, VMEM),
        name="text_gradient",
    )(terms, text_embed)
    return (row_loss.reshape(images), text_grad)


def solution(mesh):
    rows = P(("wide", "group"))
    return jax.shard_map(
        functools.partial(shards, mesh.shape["wide"]),
        mesh=mesh,
        in_specs=(rows, rows, P(), P(), P(), rows, rows, P(), P()),
        out_specs=(rows, rows),
        check_vma=False,
    )
```

```python
import functools

import jax
import jax.numpy as jnp
from jax import lax
from jax.experimental import pallas as pl
from jax.experimental.pallas import tpu as pltpu
from jax.sharding import PartitionSpec as P

LANES = 128
CORES = 2
NEAR = 4

VMEM = pl.BlockSpec(memory_space=pltpu.VMEM)
SMEM = pl.BlockSpec(memory_space=pltpu.SMEM)
ANY = pl.BlockSpec(memory_space=pl.ANY)


def dot(left, right):
    return jnp.dot(left, right, preferred_element_type=jnp.float32)


def row_dot(left, right):
    return lax.dot_general(
        left, right, (((1,), (1,)), ((), ())), preferred_element_type=jnp.float32
    )


def iota(shape, dim):
    return lax.broadcasted_iota(jnp.int32, shape, dim)


def start(copies):
    for copy in copies:
        copy.start()


def wait(copies):
    for copy in copies:
        copy.wait()


def put_rows(ref, first, rows):
    images, width = rows.shape
    for n in range(width // LANES):
        at = 2 * images * n + first
        ref[at : at + images] = rows[:, n * LANES : (n + 1) * LANES]


def get_rows(ref, first, images, width):
    step = 2 * images
    return jnp.concatenate(
        [ref[first + step * n : first + step * (n + 1)] for n in range(width // LANES)], axis=1
    )


def get_marks(ref, first, images, width, wide):
    row, lane = iota((images, LANES), 0), iota((images, LANES), 1)
    texts = jnp.where((lane == wide) | (lane == row + 32), 1.0, 0.0).astype(jnp.bfloat16)
    first += 2 * images * width // LANES
    return [texts, ref[first : first + images]]


def pool_kernel(*refs):
    inputs, out_ref, scratch = refs[:7], refs[7], refs[8:]
    patches_ref, key_ref, value_ref, counts_ref, labels_ref, query_ref, text_ref = scratch[:7]
    sems = scratch[7]
    images, patch_count, width = patches_ref.shape
    heads, head_size = query_ref.shape
    rows = images * patch_count
    patches_copy, value_copy, *small_copies = [
        pltpu.make_async_copy(inputs[n], scratch[n], sems.at[n]) for n in (0, 2, 3, 4, 5, 6)
    ]
    cut = width // (2 * LANES) * LANES + LANES
    key_parts = [slice(0, cut), slice(cut, width)]
    key_copies = [
        pltpu.make_async_copy(inputs[1].at[:, at], key_ref.at[:, at], sems.at[n])
        for n, at in zip((1, 7), key_parts)
    ]
    start(small_copies + [patches_copy] + key_copies)
    wait(small_copies)
    value_copy.start()
    text = text_ref[...].astype(jnp.float32)
    length = jnp.sqrt(jnp.sum(text * text, axis=-1, keepdims=True) + 1e-06)
    put_rows(out_ref, 0, (text / length).astype(jnp.bfloat16))
    lane = iota((images, LANES), 1)
    row = iota((images, LANES), 0)
    first = jnp.zeros((images, LANES), jnp.int32)
    second = jnp.zeros((images, LANES), jnp.int32)
    valid = jnp.zeros((images, patch_count, heads), jnp.int32)
    image = iota((images, patch_count, heads), 0)
    for i in range(images):
        label = labels_ref[i]
        high = lax.shift_right_logical(label, 4)
        first = jnp.where(row == i, high, first)
        second = jnp.where(row == i, label - 16 * high + 32, second)
        valid = jnp.where(image == i, counts_ref[i], valid)
    place = (lane == first) | (lane == second)
    out_ref[2 * images * width // LANES :] = jnp.where(place, 1.0, 0.0).astype(jnp.bfloat16)
    valid = iota((images, patch_count, heads), 1) < valid

    column = iota((1, width), 1)
    head_of = jnp.zeros((1, width), jnp.int32)
    for h in range(1, heads):
        head_of += (column >= h * head_size).astype(jnp.int32)
    inner = column - head_of * head_size
    spread = jnp.where(iota((head_size, width), 0) == inner, 1.0, 0.0).astype(jnp.bfloat16)
    own = iota((heads, width), 0) == head_of
    query = jnp.where(own, dot(query_ref[...], spread), 0.0).astype(jnp.bfloat16)
    own = jnp.where(own, 1.0, 0.0).astype(jnp.bfloat16)

    patches_copy.wait()
    flat = patches_ref[...].reshape(rows, width)
    scores = jnp.zeros((rows, heads), jnp.float32)
    for at, copy in zip(key_parts, key_copies):
        copy.wait()
        keys = dot(flat, key_ref[:, at]).astype(jnp.bfloat16)
        scores += row_dot(keys, query[:, at])
    value_copy.wait()
    values = dot(flat, value_ref[...]).astype(jnp.bfloat16)
    scores = (scores * (1.0 / head_size**0.5)).reshape(images, patch_count, heads)
    scores = jnp.where(valid, scores, -1e30)
    scores = jnp.exp(scores - jnp.max(scores, axis=1, keepdims=True))
    attend = scores / jnp.sum(scores, axis=1, keepdims=True)
    attend = attend.reshape(rows, heads).astype(jnp.bfloat16)
    terms = dot(attend, own) * values.astype(jnp.float32)
    pooled = jnp.sum(terms.reshape(images, patch_count, width), axis=1)
    pooled = pooled.astype(jnp.bfloat16).astype(jnp.float32)
    length = jnp.sqrt(jnp.sum(pooled * pooled, axis=-1, keepdims=True) + 1e-06)
    put_rows(out_ref, images, (pooled / length).astype(jnp.bfloat16))


def pair_kernel(images, width, own_ref, other_ref, scale_ref, bias_ref, out_ref):
    wide = lax.axis_index("wide")
    core = wide & (CORES - 1)
    scale, bias = scale_ref[0], bias_ref[0]
    for this, (near_ref, far_ref) in enumerate(((own_ref, other_ref), (other_ref, own_ref))):
        pl.when(core == this)(
            functools.partial(
                pair_terms, images, width, wide, this, near_ref, far_ref, scale, bias, out_ref
            )
        )


def pair_terms(images, width, wide, core, near_ref, far_ref, scale, bias, out_ref):
    size = 2 * images * width // LANES + images
    block = CORES * NEAR
    near_blocks = [
        (near_ref, (CORES * n + core) * size, (wide & ~(block - 1)) + CORES * n + core)
        for n in range(NEAR)
    ]
    far_blocks = [
        (far_ref, n * size, (wide & (block - CORES)) + n // CORES * block + n % CORES)
        for n in range(far_ref.shape[0] // size)
    ]
    near_rows, far_rows = (
        jnp.concatenate([get_rows(ref, at, images, width) for ref, at, _ in blocks])
        for blocks in (near_blocks, far_blocks)
    )
    near_marks, far_marks = (
        jnp.concatenate(sum((get_marks(ref, at, images, width, w) for ref, at, w in blocks), []))
        for blocks in (near_blocks, far_blocks)
    )
    near, far = near_rows.shape[0], far_rows.shape[0]
    raw = row_dot(near_rows, far_rows)
    match = row_dot(near_marks, far_marks)
    sign = jnp.where(match > 1.5, 1.0, -1.0)
    logits = -sign * (scale * raw + bias)
    small = jnp.exp(-jnp.abs(logits))
    softplus = jnp.maximum(logits, 0.0) + jnp.log1p(small)
    slope = -sign * (jnp.where(logits >= 0.0, 1.0, small) / (1.0 + small))
    far_is_text = (iota((near, far), 1) & images) == 0
    loss = jnp.sum(jnp.where(far_is_text, softplus, 0.0), axis=-1, keepdims=True)
    slope = jnp.where(far_is_text, 0.0, slope)
    slope = slope.reshape(NEAR, 2 * images, far)[:, :images].reshape(NEAR * images, far)
    loss = loss.reshape(NEAR, 2 * images, 1)[:, images:].reshape(NEAR * images, 1)
    high = slope.astype(jnp.bfloat16)
    low = (slope - high.astype(jnp.float32)).astype(jnp.bfloat16)
    grad = scale * (dot(high, far_rows) + dot(low, far_rows))
    lane = iota((NEAR * images, LANES), 1)
    parts = jnp.zeros((NEAR * images, LANES), jnp.float32)
    for n in range(3):
        part = loss.astype(jnp.bfloat16).astype(jnp.float32)
        parts = jnp.where(lane == n, part, parts)
        loss = loss - part
    out_ref[:, :width] = grad.astype(jnp.bfloat16)
    out_ref[:, width:] = parts.astype(jnp.bfloat16)


def grad_kernel(terms_ref, text_ref, loss_ref, grad_ref):
    images, width = text_ref.shape
    terms = terms_ref[...].astype(jnp.float32).reshape(NEAR, images, width + LANES)
    terms = jnp.sum(terms, axis=0)
    loss = jnp.sum(terms[:, width:], axis=-1, keepdims=True)
    diagonal = iota((images, images), 0) == iota((images, images), 1)
    loss_ref[...] = jnp.sum(jnp.where(diagonal, loss, 0.0), axis=0, keepdims=True)
    text = text_ref[...].astype(jnp.float32)
    length = jnp.sqrt(jnp.sum(text * text, axis=-1, keepdims=True) + 1e-06)
    unit = text / length
    grad = terms[:, :width]
    along = jnp.sum(grad * unit, axis=-1, keepdims=True)
    grad_ref[...] = (grad - along * unit) / length


def shards(
    wide, patches, counts, key_weight, value_weight, probe_query, text_embed, labels,
    logit_scale, logit_bias,
):
    images, _, width = patches.shape
    block = NEAR * CORES
    near = [
        [first + core + CORES * chip for chip in range(NEAR)]
        for first in range(0, wide, block)
        for core in range(CORES)
    ]
    cores = [[first, first + 1] for first in range(0, wide, CORES)]
    far = [
        [first + CORES * chip + 1 for first in range(0, wide, block)] for chip in range(NEAR)
    ]
    mixed = near[::CORES] + far
    arrays = (patches, key_weight, value_weight, counts, labels, probe_query, text_embed)
    places = (pltpu.VMEM,) * 3 + (pltpu.SMEM,) * 2 + (pltpu.VMEM,) * 2
    rows = pl.pallas_call(
        pool_kernel,
        out_shape=jax.ShapeDtypeStruct(
            (2 * images * width // LANES + images, LANES), jnp.bfloat16
        ),
        in_specs=[ANY] * 7,
        out_specs=VMEM,
        scratch_shapes=[place(a.shape, a.dtype) for place, a in zip(places, arrays)]
        + [pltpu.SemaphoreType.DMA((8,))],
        compiler_params=pltpu.CompilerParams(vmem_limit_bytes=60 * 2**20),
        name="pool_rows",
    )(*arrays)
    rows = lax.all_gather(rows, "wide", axis=0, tiled=True, axis_index_groups=cores)
    rows = lax.all_gather(rows, "wide", axis=0, tiled=True, axis_index_groups=mixed)
    other_rows = lax.ppermute(rows, "wide", [(i, i ^ 1) for i in range(wide)])
    terms = pl.pallas_call(
        functools.partial(pair_kernel, images, width),
        out_shape=jax.ShapeDtypeStruct((NEAR * images, width + LANES), jnp.bfloat16),
        in_specs=[VMEM] * 2 + [SMEM] * 2,
        out_specs=VMEM,
        compiler_params=pltpu.CompilerParams(vmem_limit_bytes=32 * 2**20),
        name="pair_terms",
    )(rows, other_rows, logit_scale.reshape(1), logit_bias.reshape(1))
    terms = lax.all_to_all(terms, "wide", 0, 0, tiled=True, axis_index_groups=near)
    row_loss, text_grad = pl.pallas_call(
        grad_kernel,
        out_shape=(
            jax.ShapeDtypeStruct((1, images), jnp.float32),
            jax.ShapeDtypeStruct((images, width), jnp.float32),
        ),
        in_specs=[VMEM, VMEM],
        out_specs=(VMEM, VMEM),
        compiler_params=pltpu.CompilerParams(vmem_limit_bytes=32 * 2**20),
        name="text_gradient",
    )(terms, text_embed)
    return (row_loss.reshape(images), text_grad)


def solution(mesh):
    rows = P(("wide", "group"))
    return jax.shard_map(
        functools.partial(shards, mesh.shape["wide"]),
        mesh=mesh,
        in_specs=(rows, rows, P(), P(), P(), rows, rows, P(), P()),
        out_specs=(rows, rows),
        check_vma=False,
    )
```

```python
import functools

import jax
import jax.numpy as jnp
from jax import lax
from jax.experimental import pallas as pl
from jax.experimental.pallas import tpu as pltpu
from jax.sharding import PartitionSpec as P

LANES = 128
CORES = 2
NEAR = 4

VMEM = pl.BlockSpec(memory_space=pltpu.VMEM)
SMEM = pl.BlockSpec(memory_space=pltpu.SMEM)
ANY = pl.BlockSpec(memory_space=pl.ANY)


def dot(left, right):
    return jnp.dot(left, right, preferred_element_type=jnp.float32)


def row_dot(left, right):
    return lax.dot_general(
        left, right, (((1,), (1,)), ((), ())), preferred_element_type=jnp.float32
    )


def iota(shape, dim):
    return lax.broadcasted_iota(jnp.int32, shape, dim)


def start(copies):
    for copy in copies:
        copy.start()


def wait(copies):
    for copy in copies:
        copy.wait()


def put_rows(ref, first, rows):
    images, width = rows.shape
    for n in range(width // LANES):
        at = 2 * images * n + first
        ref[at : at + images] = rows[:, n * LANES : (n + 1) * LANES]


def get_rows(ref, first, images, width):
    step = 2 * images
    return jnp.concatenate(
        [ref[first + step * n : first + step * (n + 1)] for n in range(width // LANES)], axis=1
    )


def get_marks(ref, first, images, width, wide):
    row, lane = iota((images, LANES), 0), iota((images, LANES), 1)
    texts = jnp.where((lane == wide) | (lane == row + 32), 1.0, 0.0).astype(jnp.bfloat16)
    first += 2 * images * width // LANES
    return [texts, ref[first : first + images]]


def pool_kernel(*refs):
    inputs, out_ref, scratch = refs[:7], refs[7], refs[8:]
    patches_ref, key_ref, value_ref, counts_ref, labels_ref, query_ref, text_ref = scratch[:7]
    sems = scratch[7]
    images, patch_count, width = patches_ref.shape
    heads, head_size = query_ref.shape
    rows = images * patch_count
    patches_copy, value_copy, *small_copies = [
        pltpu.make_async_copy(inputs[n], scratch[n], sems.at[n]) for n in (0, 2, 3, 4, 5, 6)
    ]
    cut = width // (2 * LANES) * LANES + LANES
    key_parts = [slice(0, cut), slice(cut, width)]
    key_copies = [
        pltpu.make_async_copy(inputs[1].at[:, at], key_ref.at[:, at], sems.at[n])
        for n, at in zip((1, 7), key_parts)
    ]
    start(small_copies + [patches_copy] + key_copies)
    wait(small_copies)
    value_copy.start()
    text = text_ref[...].astype(jnp.float32)
    length = jnp.sqrt(jnp.sum(text * text, axis=-1, keepdims=True) + 1e-06)
    put_rows(out_ref, 0, (text / length).astype(jnp.bfloat16))
    lane = iota((images, LANES), 1)
    row = iota((images, LANES), 0)
    first = jnp.zeros((images, LANES), jnp.int32)
    second = jnp.zeros((images, LANES), jnp.int32)
    valid = jnp.zeros((images, patch_count, heads), jnp.int32)
    image = iota((images, patch_count, heads), 0)
    for i in range(images):
        label = labels_ref[i]
        high = lax.shift_right_logical(label, 4)
        first = jnp.where(row == i, high, first)
        second = jnp.where(row == i, label - 16 * high + 32, second)
        valid = jnp.where(image == i, counts_ref[i], valid)
    place = (lane == first) | (lane == second)
    out_ref[2 * images * width // LANES :] = jnp.where(place, 1.0, 0.0).astype(jnp.bfloat16)
    valid = iota((images, patch_count, heads), 1) < valid

    column = iota((1, width), 1)
    head_of = jnp.zeros((1, width), jnp.int32)
    for h in range(1, heads):
        head_of += (column >= h * head_size).astype(jnp.int32)
    inner = column - head_of * head_size
    spread = jnp.where(iota((head_size, width), 0) == inner, 1.0, 0.0).astype(jnp.bfloat16)
    own = iota((heads, width), 0) == head_of
    query = jnp.where(own, dot(query_ref[...], spread), 0.0).astype(jnp.bfloat16)
    own = jnp.where(own, 1.0, 0.0).astype(jnp.bfloat16)

    patches_copy.wait()
    flat = patches_ref[...].reshape(rows, width)
    scores = jnp.zeros((rows, heads), jnp.float32)
    for at, copy in zip(key_parts, key_copies):
        copy.wait()
        keys = dot(flat, key_ref[:, at]).astype(jnp.bfloat16)
        scores += row_dot(keys, query[:, at])
    value_copy.wait()
    values = dot(flat, value_ref[...])
    scores = (scores * (1.0 / head_size**0.5)).reshape(images, patch_count, heads)
    scores = jnp.where(valid, scores, -1e30)
    scores = jnp.exp(scores - jnp.max(scores, axis=1, keepdims=True))
    attend = scores / jnp.sum(scores, axis=1, keepdims=True)
    attend = attend.reshape(rows, heads).astype(jnp.bfloat16)
    terms = dot(attend, own) * values
    pooled = jnp.sum(terms.reshape(images, patch_count, width), axis=1)
    pooled = pooled.astype(jnp.bfloat16).astype(jnp.float32)
    length = jnp.sqrt(jnp.sum(pooled * pooled, axis=-1, keepdims=True) + 1e-06)
    put_rows(out_ref, images, (pooled / length).astype(jnp.bfloat16))


def pair_kernel(images, width, own_ref, other_ref, scale_ref, bias_ref, out_ref):
    wide = lax.axis_index("wide")
    core = wide & (CORES - 1)
    scale, bias = scale_ref[0], bias_ref[0]
    for this, (near_ref, far_ref) in enumerate(((own_ref, other_ref), (other_ref, own_ref))):
        pl.when(core == this)(
            functools.partial(
                pair_terms, images, width, wide, this, near_ref, far_ref, scale, bias, out_ref
            )
        )


def pair_terms(images, width, wide, core, near_ref, far_ref, scale, bias, out_ref):
    size = 2 * images * width // LANES + images
    block = CORES * NEAR
    near_blocks = [
        (near_ref, (CORES * n + core) * size, (wide & ~(block - 1)) + CORES * n + core)
        for n in range(NEAR)
    ]
    far_blocks = [
        (far_ref, n * size, (wide & (block - CORES)) + n // CORES * block + n % CORES)
        for n in range(far_ref.shape[0] // size)
    ]
    near_rows, far_rows = (
        jnp.concatenate([get_rows(ref, at, images, width) for ref, at, _ in blocks])
        for blocks in (near_blocks, far_blocks)
    )
    near_marks, far_marks = (
        jnp.concatenate(sum((get_marks(ref, at, images, width, w) for ref, at, w in blocks), []))
        for blocks in (near_blocks, far_blocks)
    )
    near, far = near_rows.shape[0], far_rows.shape[0]
    raw = row_dot(near_rows, far_rows)
    match = row_dot(near_marks, far_marks)
    sign = jnp.where(match > 1.5, 1.0, -1.0)
    logits = -sign * (scale * raw + bias)
    small = jnp.exp(-jnp.abs(logits))
    softplus = jnp.maximum(logits, 0.0) + jnp.log1p(small)
    slope = -sign * (jnp.where(logits >= 0.0, 1.0, small) / (1.0 + small))
    far_is_text = (iota((near, far), 1) & images) == 0
    loss = jnp.sum(jnp.where(far_is_text, softplus, 0.0), axis=-1, keepdims=True)
    slope = jnp.where(far_is_text, 0.0, slope)
    slope = slope.reshape(NEAR, 2 * images, far)[:, :images].reshape(NEAR * images, far)
    loss = loss.reshape(NEAR, 2 * images, 1)[:, images:].reshape(NEAR * images, 1)
    high = slope.astype(jnp.bfloat16)
    low = (slope - high.astype(jnp.float32)).astype(jnp.bfloat16)
    grad = scale * (dot(high, far_rows) + dot(low, far_rows))
    lane = iota((NEAR * images, LANES), 1)
    parts = jnp.zeros((NEAR * images, LANES), jnp.float32)
    for n in range(3):
        part = loss.astype(jnp.bfloat16).astype(jnp.float32)
        parts = jnp.where(lane == n, part, parts)
        loss = loss - part
    out_ref[:, :width] = grad.astype(jnp.bfloat16)
    out_ref[:, width:] = parts.astype(jnp.bfloat16)


def grad_kernel(terms_ref, text_ref, loss_ref, grad_ref):
    images, width = text_ref.shape
    terms = terms_ref[...].astype(jnp.float32).reshape(NEAR, images, width + LANES)
    terms = jnp.sum(terms, axis=0)
    loss = jnp.sum(terms[:, width:], axis=-1, keepdims=True)
    diagonal = iota((images, images), 0) == iota((images, images), 1)
    loss_ref[...] = jnp.sum(jnp.where(diagonal, loss, 0.0), axis=0, keepdims=True)
    text = text_ref[...].astype(jnp.float32)
    length = jnp.sqrt(jnp.sum(text * text, axis=-1, keepdims=True) + 1e-06)
    unit = text / length
    grad = terms[:, :width]
    along = jnp.sum(grad * unit, axis=-1, keepdims=True)
    grad_ref[...] = (grad - along * unit) / length


def shards(
    wide, patches, counts, key_weight, value_weight, probe_query, text_embed, labels,
    logit_scale, logit_bias,
):
    images, _, width = patches.shape
    block = NEAR * CORES
    near = [
        [first + core + CORES * chip for chip in range(NEAR)]
        for first in range(0, wide, block)
        for core in range(CORES)
    ]
    cores = [[first, first + 1] for first in range(0, wide, CORES)]
    far = [
        [first + CORES * chip + 1 for first in range(0, wide, block)] for chip in range(NEAR)
    ]
    mixed = near[::CORES] + far
    arrays = (patches, key_weight, value_weight, counts, labels, probe_query, text_embed)
    places = (pltpu.VMEM,) * 3 + (pltpu.SMEM,) * 2 + (pltpu.VMEM,) * 2
    rows = pl.pallas_call(
        pool_kernel,
        out_shape=jax.ShapeDtypeStruct(
            (2 * images * width // LANES + images, LANES), jnp.bfloat16
        ),
        in_specs=[ANY] * 7,
        out_specs=VMEM,
        scratch_shapes=[place(a.shape, a.dtype) for place, a in zip(places, arrays)]
        + [pltpu.SemaphoreType.DMA((8,))],
        compiler_params=pltpu.CompilerParams(vmem_limit_bytes=60 * 2**20),
        name="pool_rows",
    )(*arrays)
    rows = lax.all_gather(rows, "wide", axis=0, tiled=True, axis_index_groups=cores)
    rows = lax.all_gather(rows, "wide", axis=0, tiled=True, axis_index_groups=mixed)
    other_rows = lax.ppermute(rows, "wide", [(i, i ^ 1) for i in range(wide)])
    terms = pl.pallas_call(
        functools.partial(pair_kernel, images, width),
        out_shape=jax.ShapeDtypeStruct((NEAR * images, width + LANES), jnp.bfloat16),
        in_specs=[VMEM] * 2 + [SMEM] * 2,
        out_specs=VMEM,
        compiler_params=pltpu.CompilerParams(vmem_limit_bytes=32 * 2**20),
        name="pair_terms",
    )(rows, other_rows, logit_scale.reshape(1), logit_bias.reshape(1))
    terms = lax.all_to_all(terms, "wide", 0, 0, tiled=True, axis_index_groups=near)
    row_loss, text_grad = pl.pallas_call(
        grad_kernel,
        out_shape=(
            jax.ShapeDtypeStruct((1, images), jnp.float32),
            jax.ShapeDtypeStruct((images, width), jnp.float32),
        ),
        in_specs=[VMEM, VMEM],
        out_specs=(VMEM, VMEM),
        compiler_params=pltpu.CompilerParams(vmem_limit_bytes=32 * 2**20),
        name="text_gradient",
    )(terms, text_embed)
    return (row_loss.reshape(images), text_grad)


def solution(mesh):
    rows = P(("wide", "group"))
    return jax.shard_map(
        functools.partial(shards, mesh.shape["wide"]),
        mesh=mesh,
        in_specs=(rows, rows, P(), P(), P(), rows, rows, P(), P()),
        out_specs=(rows, rows),
        check_vma=False,
    )
```
